1024 devices in a mesh: row: 128 (over z, x, core), col: 8 (over y).
Axes of the slice: x: 4, y: 8, z: 16, core: 2. Of those that a mesh axis runs over, the one named last changes fastest.
Arguments:
- features: bfloat16 [131072, 256], P(('row', 'col')), may hold values from -6 to 6
- self_weight: bfloat16 [256, 256], replicated, may hold values from -0.375 to 0.375
- neigh_weight: bfloat16 [256, 256], replicated, may hold values from -0.375 to 0.375
- tiles: bfloat16 [128, 8, 16, 128, 128], P('row', 'col'), may hold values from 0 to 1
- tile_rows: int32 [128, 8, 16], P('row', 'col'), may hold values from 0 to 7
- tile_bands: int32 [128, 8, 16], P('row', 'col'), may hold values from 0 to 4
- tile_count: int32 [128, 8], P('row', 'col'), may hold values from 1 to 16, as said below
- degree: int32 [131072], P(('row', 'col')), may hold values from 16 to 96
- cotangent: bfloat16 [131072, 256], P(('row', 'col')), may hold values from -6 to 6
Outputs:
- output: bfloat16 [131072, 256], P(('row', 'col'))
- feature_grad: bfloat16 [131072, 256], P(('row', 'col'))
- self_grad: float32 [256, 256], replicated
- neigh_grad: float32 [256, 256], replicated
The draws below stay inside these ranges and needn't reach their ends.
Inputs may be any that keep to these rules, and one draw needn't show every extreme that they name: `tile_count`: some device uses all 16 slots.
All inputs are finite; a program needn't handle non-finite values.
Results may differ from the reference program's by a relative error of at most 0.017.
Values may be sent and summed in bfloat16 or wider, within the bound.
No kernel may reach another device: no remote copies, remote signals or barrier semaphores. Data moves between devices by JAX's collectives and lax.ppermute only.
A program may use at most 32 MiB of HBM per device.

```python
import jax
import jax.numpy as jnp
from jax import lax

F = 256
BLK = 128
TILES = 16
HALO = 2
NODES = 131072
N_ROW = 128
N_COL = 8


def draw_tile_count(key, part):
    key = jax.random.fold_in(key, 7)
    first, second, third, fourth = jax.random.split(key, 4)
    base = jax.random.randint(first, (N_ROW, N_COL), max(1, TILES // 6), TILES // 2 + 1)
    heavy = jax.random.randint(second, (N_ROW, N_COL), 0, 12) == 0
    high = jax.random.randint(third, (N_ROW, N_COL), 3 * TILES // 4, TILES + 1)
    counts = jnp.where(heavy, high, base)
    where_full = jax.random.randint(fourth, (), 0, N_ROW * N_COL)
    flat = jnp.arange(N_ROW * N_COL, dtype=jnp.int32).reshape(N_ROW, N_COL)
    return jnp.where(flat == where_full, TILES, counts).astype(jnp.int32)


def place_ends(values, rng, low, largest):
    longest = values.shape.index(max(values.shape))
    spots = []
    for shift in (0, 1):
        where = [jax.random.randint(jax.random.fold_in(rng, axis), (), 0, length) for axis, length in enumerate(values.shape)]
        where[longest] = (where[longest] + shift) % values.shape[longest]
        spots.append(tuple(where))
    return values.at[spots[0]].set(low).at[spots[1]].set(largest)


def levels(own_key, extent, cuts, least, top_value):
    def one(position, shards_of):
        steps = jax.random.uniform(jax.random.fold_in(jax.random.fold_in(own_key, 6), position), (shards_of,), jnp.float32, least / len(cuts), top_value / len(cuts))
        return jnp.repeat(jnp.exp(steps), extent[position] // shards_of).reshape((-1,) + (1,) * (len(extent) - position - 1))

    factor_of = one(*cuts[0])
    for cut in cuts[1:]:
        factor_of = factor_of * one(*cut)
    return factor_of


def centred(rng, shape, width, bound, cuts=(), held_as=jnp.bfloat16):
    result = width * jax.random.normal(rng, shape, jnp.float32)
    if cuts:
        result = result * levels(rng, shape, cuts, -0.22, 0.18)
    return jnp.clip(result, -bound, bound).astype(held_as)


def setup_inputs(seed: int = 0) -> dict:
    seeds = jax.random.split(jax.random.key(seed), 10)
    features = centred(seeds[0], (NODES, F), 1.0, 6.0, ((0, 1024),))
    self_weight = centred(seeds[1], (F, F), F ** -0.5, 0.375)
    neigh_weight = centred(seeds[2], (F, F), F ** -0.5, 0.375)
    tiles = jnp.clip(1.0 * jax.random.uniform(seeds[3], (N_ROW, N_COL, TILES, BLK, BLK), jnp.float32) ** levels(seeds[3], (N_ROW, N_COL, TILES, BLK, BLK), ((0, 128), (1, 8)), -0.2, 0.2), 0.0, 1.0).astype(jnp.bfloat16)
    tile_rows = place_ends(jax.random.randint(seeds[4], (N_ROW, N_COL, TILES), 0, N_COL), jax.random.fold_in(seeds[4], 1), 0, N_COL - 1).astype(jnp.int32)
    tile_bands = place_ends(jax.random.randint(seeds[5], (N_ROW, N_COL, TILES), 0, 2 * HALO + 1), jax.random.fold_in(seeds[5], 1), 0, 2 * HALO).astype(jnp.int32)
    tile_count = draw_tile_count(jax.random.fold_in(seeds[9], 71), 0)
    degree = place_ends(jax.random.randint(seeds[7], (NODES,), 16, 97), jax.random.fold_in(seeds[7], 1), 16, 96).astype(jnp.int32)
    cotangent = centred(seeds[8], (NODES, F), 1.0, 6.0, ((0, 1024),))
    return dict(features=features, self_weight=self_weight, neigh_weight=neigh_weight, tiles=tiles, tile_rows=tile_rows, tile_bands=tile_bands, tile_count=tile_count, degree=degree, cotangent=cotangent)


def to_half(values):
    rounded = lax.optimization_barrier(values.astype(jnp.bfloat16))
    return rounded.astype(jnp.float32)

def reference(features, self_weight, neigh_weight, tiles, tile_rows, tile_bands, tile_count, degree, cotangent):
    wide = 2 * HALO + 1
    blocks = features.reshape(N_ROW, N_COL, BLK, F)
    padded = jnp.pad(blocks, ((HALO, HALO), (0, 0), (0, 0), (0, 0)))
    slots = jnp.arange(TILES, dtype=jnp.int32)
    columns = jnp.arange(N_COL, dtype=jnp.int32)
    offsets = jnp.arange(wide, dtype=jnp.int32)

    def band_sum(band):
        window = lax.dynamic_slice_in_dim(padded, band, wide, 0)
        window = jnp.transpose(window, (1, 0, 2, 3))
        tile_band = tiles[band].astype(jnp.float32)
        live = slots[None, :] < tile_count[band][:, None]
        picked = jax.vmap(lambda w, b: w[b])(window, tile_bands[band]).astype(jnp.float32)
        product = jnp.einsum('ctab,ctbf->ctaf', tile_band, picked)
        select = ((tile_rows[band][..., None] == columns) & live[..., None]).astype(jnp.float32)
        per_device = to_half(jnp.einsum('cti,ctaf->ciaf', select, product))
        return lax.optimization_barrier(jnp.sum(per_device, axis=0))
    sums = lax.map(band_sum, jnp.arange(N_ROW, dtype=jnp.int32)).reshape(NODES, F)
    norm = degree.astype(jnp.float32)[:, None]
    aggregate = (sums / norm).astype(jnp.bfloat16)
    output = (jnp.dot(features, self_weight, preferred_element_type=jnp.float32) + jnp.dot(aggregate, neigh_weight, preferred_element_type=jnp.float32)).astype(jnp.bfloat16)
    scaled = (jnp.dot(cotangent, neigh_weight.T, preferred_element_type=jnp.float32) / norm).astype(jnp.bfloat16)
    scaled_blocks = scaled.reshape(N_ROW, N_COL, BLK, F)

    def spread_band(total, band):
        tile_band = tiles[band].astype(jnp.float32)
        live = slots[None, :] < tile_count[band][:, None]
        gathered = scaled_blocks[band][tile_rows[band]].astype(jnp.float32)
        contrib = jnp.einsum('ctab,ctaf->ctbf', tile_band, gathered)
        select = ((tile_bands[band][..., None] == offsets) & live[..., None]).astype(jnp.float32)
        landed = to_half(jnp.einsum('ctw,ctbf->wcbf', select, contrib))
        current = lax.dynamic_slice_in_dim(total, band, wide, 0)
        return (lax.dynamic_update_slice_in_dim(total, current + landed, band, 0), None)
    start = jnp.zeros((N_ROW + 2 * HALO, N_COL, BLK, F), jnp.float32)
    total, unused = lax.scan(spread_band, start, jnp.arange(N_ROW, dtype=jnp.int32))
    spread = total[HALO:HALO + N_ROW].reshape(NODES, F)
    feature_grad = (jnp.dot(cotangent, self_weight.T, preferred_element_type=jnp.float32) + spread).astype(jnp.bfloat16)
    factor = 1.0 / jnp.sqrt(jnp.float32(NODES))
    self_grad = jnp.dot(features.T, cotangent, preferred_element_type=jnp.float32) * factor
    neigh_grad = jnp.dot(aggregate.T, cotangent, preferred_element_type=jnp.float32) * factor
    return (output, feature_grad, self_grad, neigh_grad)
```

```python
import functools
import math

import jax
import jax.numpy as jnp
import numpy as np
from jax import lax
from jax.experimental import pallas as pl
from jax.experimental.pallas import tpu as pltpu
from jax.sharding import Mesh
from jax.sharding import PartitionSpec as P

HALO = 2
WIDE = 2 * HALO + 1
ROW = ("z", "x", "core")
NEAR = ("x", "core", "y")
LIMIT = 48 * 1024 * 1024

VM = pl.BlockSpec(memory_space=pltpu.VMEM)
SM = pl.BlockSpec(memory_space=pltpu.SMEM)
HB = pl.BlockSpec(memory_space=pl.ANY)


def call(body, outs, in_specs, out_specs=None, scratch=(), aliases=None, cost=None):
    return pl.pallas_call(
        body,
        out_shape=outs,
        in_specs=in_specs,
        out_specs=out_specs if out_specs is not None else jax.tree.map(lambda _: VM, outs),
        scratch_shapes=list(scratch),
        input_output_aliases=aliases or {},
        cost_estimate=cost,
        compiler_params=pltpu.CompilerParams(vmem_limit_bytes=LIMIT),
    )


def half(*shape):
    return jax.ShapeDtypeStruct(shape, jnp.bfloat16)


def full(*shape):
    return jax.ShapeDtypeStruct(shape, jnp.float32)


def dot(a, b, ca, cb):
    return lax.dot_general(a, b, (((ca,), (cb,)), ((), ())), preferred_element_type=jnp.float32)


def cost(flops, moved):
    return pl.CostEstimate(flops=flops, bytes_accessed=moved, transcendentals=0)


def pair_body(spot, own, below, above, out):
    blk = own.shape[0]
    out[:blk, :] = own[...]
    out[blk:, :] = jnp.where(spot[0] == 0, above[...], below[...])


def forward_body(rows, bands, count, spot, tiles, f0, near, f4, own, out, sent, kept, window, total):
    slots, blk = tiles.shape[0], tiles.shape[1]
    ncol = total.shape[0] - 1
    core = spot[0]
    window[0] = f0[...]
    window[1] = near[pl.ds(pl.multiple_of((1 - core) * blk, blk), blk), :]
    window[2] = own[...]
    window[3] = near[pl.ds(pl.multiple_of(core * blk, blk), blk), :]
    window[4] = f4[...]
    total[...] = jnp.zeros_like(total)
    for slot in range(slots):
        place = jnp.where(slot < count[0], rows[slot], ncol)
        total[place] += dot(tiles[slot], window[bands[slot]], 1, 0)
    for at in range(ncol):
        out[at * blk : (at + 1) * blk, :] = total[at].astype(jnp.bfloat16)
    bit = spot[1]
    for at in range(ncol // 2):
        sent[at * blk : (at + 1) * blk, :] = total[2 * at + 1 - bit].astype(jnp.bfloat16)
        kept[at * blk : (at + 1) * blk, :] = total[2 * at + bit].astype(jnp.bfloat16)


def halve_body(blk, which):
    def body(spot, came, held, sent, kept):
        bit = spot[which]
        for at in range(sent.shape[0] // blk):
            for out, side in ((sent, 1 - bit), (kept, bit)):
                start = pl.multiple_of((2 * at + side) * blk, blk)
                rows = pl.ds(start, blk)
                total = came[rows, :].astype(jnp.float32) + held[rows, :].astype(jnp.float32)
                out[at * blk : (at + 1) * blk, :] = total.astype(out.dtype)

    return body


def column(degree, width):
    blk = degree.shape[1]
    tall = jnp.broadcast_to(degree[...].astype(jnp.float32), (blk, blk)).T
    return jnp.concatenate([tall] * (width // blk), axis=1)


def share_body(degree, cotangent, out):
    blk, width = cotangent.shape
    share = (cotangent[...].astype(jnp.float32) / column(degree, width)).astype(jnp.bfloat16)
    for at in range(out.shape[0] // blk):
        out[at * blk : (at + 1) * blk, :] = share


def grads_body(features, cotangent, partial, shares, sent, out, passed):
    own = dot(features[...], cotangent[...], 0, 0).astype(jnp.bfloat16)
    neigh = dot(partial[...], shares[...], 0, 0).astype(jnp.bfloat16)
    height, lanes = own.shape[0], out.shape[1]
    for at in range(2):
        out[at * height : (at + 1) * height, :] = own[:, at * lanes : (at + 1) * lanes]
        out[(at + 2) * height : (at + 3) * height, :] = neigh[:, at * lanes : (at + 1) * lanes]


def backward_body(rows, bands, count, tiles, shares, weight, after, far0, near, own, far1, total):
    slots, blk = tiles.shape[0], tiles.shape[1]
    total[...] = jnp.zeros_like(total)
    for slot in range(slots):
        place = jnp.where(slot < count[0], bands[slot], WIDE)
        start = pl.multiple_of(rows[slot] * blk, blk)
        total[place] += dot(tiles[slot], shares[pl.ds(start, blk), :], 0, 0)
    landed = [
        dot(total[at].astype(jnp.bfloat16), weight[...], 1, 1).astype(jnp.bfloat16)
        for at in range(WIDE)
    ]
    far0[...], own[...], far1[...] = landed[0], landed[2], landed[4]
    near[:blk, :], near[blk:, :] = landed[1], landed[3]


def merge_body(spot, came, far0, far1, own, low, high, mid):
    blk = own.shape[0]
    core = spot[0]
    lower = came[:blk, :].astype(jnp.float32)
    upper = came[blk:, :].astype(jnp.float32)
    low[...] = jnp.where(core == 1, far0[...].astype(jnp.float32) + lower, far0[...].astype(jnp.float32)).astype(low.dtype)
    high[...] = jnp.where(core == 0, far1[...].astype(jnp.float32) + upper, far1[...].astype(jnp.float32)).astype(high.dtype)
    mid[...] = own[...].astype(jnp.float32) + jnp.where(core == 0, lower, upper)


def fold(source, members):
    rows = source.shape[0] // members
    total = source[:rows, :].astype(jnp.float32)
    for at in range(1, members):
        total = total + source[at * rows : (at + 1) * rows, :].astype(jnp.float32)
    return total


def fold_spread(value, members, copies, after=()):
    rows, lanes = value.shape[0] // members, value.shape[1]

    def body(*refs):
        total = fold(refs[0], members).astype(jnp.bfloat16)
        for at in range(copies):
            refs[-1][at * rows : (at + 1) * rows, :] = total

    return call(body, half(copies * rows, lanes), [VM] + [HB] * len(after))(value, *after)


def finish_body(factor, source, own, neigh):
    height, lanes = own.shape[0], source.shape[1]
    for at in range(2):
        for first, grad in ((at, own), (at + 2, neigh)):
            grad[:, at * lanes : (at + 1) * lanes] = (
                source[first * height : (first + 1) * height, :].astype(jnp.float32) * factor
            )


def output_body(came, held, degree, features, self_weight, neigh_weight, out):
    sums = came[...].astype(jnp.float32) + held[...]
    aggregate = (sums / column(degree, out.shape[1])).astype(jnp.bfloat16)
    out[...] = (
        dot(features[...], self_weight[...], 1, 0) + dot(aggregate, neigh_weight[...], 1, 0)
    ).astype(jnp.bfloat16)


def feature_body(low, high, mid, cotangent, self_weight, out):
    spread = mid[...] + low[...].astype(jnp.float32) + high[...].astype(jnp.float32)
    out[...] = (dot(cotangent[...], self_weight[...], 1, 1) + spread).astype(jnp.bfloat16)


def passed_along(value, steps):
    count = lax.axis_size(ROW)
    leading, last = max(0, -steps), min(count, count - steps)
    return lax.ppermute(value, ROW, [(source, source + steps) for source in range(leading, last)])


def crossed(value, axis, flip):
    return lax.ppermute(value, axis, [(at, at ^ flip) for at in range(lax.axis_size(axis))])


def exchange(value, axes):
    return lax.all_to_all(value, axes, 0, 0, tiled=True)


def local(
    features, self_weight, neigh_weight, tiles, tile_rows, tile_bands, tile_count, degree, cotangent
):
    ncol = lax.axis_size("y")
    near, far = lax.axis_size(NEAR), lax.axis_size("z")
    blk, width = features.shape
    lanes = width // 2
    slots = tiles.shape[2]
    tile_set = tiles[0, 0]
    rows, bands, count = tile_rows[0, 0], tile_bands[0, 0], tile_count[0]
    core, at_col = lax.axis_index("core"), lax.axis_index("y")
    spot = jnp.stack([core, at_col % 2, at_col // 2 % 2, at_col // 4]).astype(jnp.int32)
    degree = degree[None, :]
    work = 2 * slots * blk * blk * width
    factor = 1.0 / math.sqrt(lax.axis_size(ROW) * ncol * blk)

    copies = call(share_body, half(ncol * blk, width), [VM] * 2)(degree, cotangent)
    shares = exchange(copies, "y")
    below, above = passed_along(features, 2), passed_along(features, -2)
    pair = call(pair_body, half(2 * blk, width), [SM] + [VM] * 3)(spot, features, below, above)
    near_blocks = crossed(pair, "core", 1)
    partial, sent, kept = call(
        forward_body,
        [half(ncol * blk, width)] + [half(ncol // 2 * blk, width)] * 2,
        [SM] * 4 + [VM] * 5,
        scratch=[
            pltpu.VMEM((WIDE, blk, width), jnp.bfloat16),
            pltpu.VMEM((ncol + 1, blk, width), jnp.float32),
        ],
        cost=cost(work, tile_set.size * 2 + 21 * features.size * 2),
    )(rows, bands, count, spot, tile_set, below, near_blocks, above, features)

    grads, sent = call(
        grads_body,
        [half(4 * width, lanes), half(*sent.shape)],
        [VM] * 4 + [HB],
        [VM, HB],
        aliases={4: 1},
        cost=cost(2 * (ncol + 1) * blk * width * width, 18 * features.size * 2),
    )(features, cotangent, partial, shares, sent)
    scattered = exchange(grads, NEAR)

    far0, near_landed, own, far1 = call(
        backward_body,
        [half(blk, width), half(2 * blk, width), half(blk, width), half(blk, width)],
        [SM] * 3 + [VM] * 3 + [HB],
        scratch=[pltpu.VMEM((WIDE + 1, blk, width), jnp.float32)],
        cost=cost(work, tile_set.size * 2 + 13 * features.size * 2),
    )(rows, bands, count, tile_set, shares, neigh_weight, grads)
    near_landed = crossed(near_landed, "core", 1)
    came = crossed(sent, "y", 1)

    joined = fold_spread(scattered, near, far, after=[near_landed, came])
    joined = exchange(joined, "z")

    low, high, mid = call(
        merge_body, [half(blk, width)] * 2 + [full(blk, width)], [SM] + [VM] * 4
    )(spot, near_landed, far0, far1, own)
    low, high = passed_along(low, -2), passed_along(high, 2)
    sent, kept = call(
        halve_body(blk, 2),
        [half(ncol // 4 * blk, width), full(ncol // 4 * blk, width)],
        [SM] + [VM] * 2,
    )(spot, came, kept)
    came = crossed(sent, "y", 2)

    grads = fold_spread(joined, far, near, after=[low, high, came])
    gathered = exchange(grads, NEAR)

    feature_grad = call(feature_body, half(blk, width), [VM] * 5)(
        low, high, mid, cotangent, self_weight
    )
    sent, kept = call(halve_body(blk, 3), [half(blk, width), full(blk, width)], [SM] + [VM] * 2)(
        spot, came, kept
    )
    came = crossed(sent, "y", 4)
    output = call(output_body, half(blk, width), [VM] * 6)(
        came, kept, degree, features, self_weight, neigh_weight
    )
    self_grad, neigh_grad = call(
        functools.partial(finish_body, factor), [full(width, width)] * 2, [VM]
    )(gathered)
    return (output, feature_grad, self_grad, neigh_grad)


def solution(mesh):
    fine = Mesh(
        np.array(mesh.devices).reshape(mesh.shape["row"] // 8, 4, 2, mesh.shape["col"]),
        ROW + ("y",),
    )
    nodes = ROW + ("y",)
    in_specs = (
        P(nodes, None),
        P(),
        P(),
        P(ROW, "y", None, None, None),
        P(ROW, "y", None),
        P(ROW, "y", None),
        P(ROW, "y"),
        P(nodes),
        P(nodes, None),
    )
    out_specs = (P(nodes, None), P(nodes, None), P(), P())
    return jax.shard_map(local, mesh=fine, in_specs=in_specs, out_specs=out_specs, check_vma=False)
```

```python
import functools
import math

import jax
import jax.numpy as jnp
import numpy as np
from jax import lax
from jax.experimental import pallas as pl
from jax.experimental.pallas import tpu as pltpu
from jax.sharding import Mesh
from jax.sharding import PartitionSpec as P

HALO = 2
WIDE = 2 * HALO + 1
ROW = ("z", "x", "core")
NEAR = ("x", "core", "y")
LIMIT = 48 * 1024 * 1024

VM = pl.BlockSpec(memory_space=pltpu.VMEM)
SM = pl.BlockSpec(memory_space=pltpu.SMEM)
HB = pl.BlockSpec(memory_space=pl.ANY)


def call(body, outs, in_specs, scratch=(), cost=None):
    return pl.pallas_call(
        body,
        out_shape=outs,
        in_specs=in_specs,
        out_specs=[VM] * len(outs) if isinstance(outs, list) else VM,
        scratch_shapes=list(scratch),
        cost_estimate=cost,
        compiler_params=pltpu.CompilerParams(vmem_limit_bytes=LIMIT),
    )


def half(*shape):
    return jax.ShapeDtypeStruct(shape, jnp.bfloat16)


def full(*shape):
    return jax.ShapeDtypeStruct(shape, jnp.float32)


def dot(a, b, ca, cb):
    return lax.dot_general(a, b, (((ca,), (cb,)), ((), ())), preferred_element_type=jnp.float32)


def cost(flops, moved):
    return pl.CostEstimate(flops=flops, bytes_accessed=moved, transcendentals=0)


def pair_body(spot, own, below, above, out):
    blk = own.shape[0]
    out[:blk, :] = own[...]
    out[blk:, :] = jnp.where(spot[0] == 0, above[...], below[...])


def lay_out(window, spot, f0, pair, own, f4):
    blk = own.shape[0]
    core = spot[0]
    window[0] = f0[...]
    window[1 + 2 * (1 - core)] = pair[:blk, :]
    window[2] = own[...]
    window[1 + 2 * core] = pair[blk:, :]
    window[4] = f4[...]


def forward_body(rows, bands, count, spot, tiles, window, after, sent, kept, total):
    slots, blk = tiles.shape[0], tiles.shape[1]
    ncol = total.shape[0] - 1
    total[...] = jnp.zeros_like(total)
    for slot in range(slots):
        place = jnp.where(slot < count[0], rows[slot], ncol)
        total[place] += dot(tiles[slot], window[bands[slot]], 1, 0)
    bit = spot[1]
    for at in range(ncol // 2):
        sent[at * blk : (at + 1) * blk, :] = total[2 * at + 1 - bit].astype(jnp.bfloat16)
        kept[at * blk : (at + 1) * blk, :] = total[2 * at + bit].astype(jnp.bfloat16)


def halve_body(blk, which):
    def body(spot, came, held, *rest):
        sent, kept = rest[-2:]
        bit = spot[which]
        for at in range(sent.shape[0] // blk):
            for out, side in ((sent, 1 - bit), (kept, bit)):
                start = pl.multiple_of((2 * at + side) * blk, blk)
                rows = pl.ds(start, blk)
                total = came[rows, :].astype(jnp.float32) + held[rows, :].astype(jnp.float32)
                out[at * blk : (at + 1) * blk, :] = total.astype(out.dtype)

    return body


def column(degree, width):
    blk = degree.shape[1]
    tall = jnp.broadcast_to(degree[...].astype(jnp.float32), (blk, blk)).T
    return jnp.concatenate([tall] * (width // blk), axis=1)


def share_body(degree, cotangent, out):
    blk, width = cotangent.shape
    share = (cotangent[...].astype(jnp.float32) / column(degree, width)).astype(jnp.bfloat16)
    for at in range(out.shape[0] // blk):
        out[at * blk : (at + 1) * blk, :] = share


def grads_body(spot, cotangent, f0, pair, features, f4, landing, out, window):
    lay_out(window, spot, f0, pair, features, f4)
    own = dot(features[...], cotangent[...], 0, 0).astype(jnp.bfloat16)
    neigh = dot(window[0], landing[0], 0, 0)
    for at in range(1, WIDE):
        neigh = neigh + dot(window[at], landing[at], 0, 0)
    neigh = neigh.astype(jnp.bfloat16)
    height, lanes = own.shape[0], out.shape[1]
    for at in range(2):
        out[at * height : (at + 1) * height, :] = own[:, at * lanes : (at + 1) * lanes]
        out[(at + 2) * height : (at + 3) * height, :] = neigh[:, at * lanes : (at + 1) * lanes]


def backward_body(rows, bands, count, tiles, shares, weight, out, far0, near, own, far1, total):
    slots, blk = tiles.shape[0], tiles.shape[1]
    total[...] = jnp.zeros_like(total)
    for slot in range(slots):
        place = jnp.where(slot < count[0], bands[slot], WIDE)
        start = pl.multiple_of(rows[slot] * blk, blk)
        total[place] += dot(tiles[slot], shares[pl.ds(start, blk), :], 0, 0)
    landed = []
    for at in range(WIDE):
        out[at] = total[at].astype(jnp.bfloat16)
        landed.append(dot(out[at], weight[...], 1, 1).astype(jnp.bfloat16))
    far0[...], own[...], far1[...] = landed[0], landed[2], landed[4]
    near[:blk, :], near[blk:, :] = landed[1], landed[3]


def merge_body(spot, came, far0, far1, own, low, high, mid):
    blk = own.shape[0]
    core = spot[0]
    lower = came[:blk, :].astype(jnp.float32)
    upper = came[blk:, :].astype(jnp.float32)
    low[...] = jnp.where(core == 1, far0[...].astype(jnp.float32) + lower, far0[...].astype(jnp.float32)).astype(low.dtype)
    high[...] = jnp.where(core == 0, far1[...].astype(jnp.float32) + upper, far1[...].astype(jnp.float32)).astype(high.dtype)
    mid[...] = own[...].astype(jnp.float32) + jnp.where(core == 0, lower, upper)


def fold(source, members):
    rows = source.shape[0] // members
    total = source[:rows, :].astype(jnp.float32)
    for at in range(1, members):
        total = total + source[at * rows : (at + 1) * rows, :].astype(jnp.float32)
    return total


def fold_spread(value, members, copies, after=()):
    rows, lanes = value.shape[0] // members, value.shape[1]

    def body(*refs):
        total = fold(refs[0], members).astype(jnp.bfloat16)
        for at in range(copies):
            refs[-1][at * rows : (at + 1) * rows, :] = total

    return call(body, half(copies * rows, lanes), [VM] + [HB] * len(after))(value, *after)


def finish_body(factor, source, own, neigh):
    height, lanes = own.shape[0], source.shape[1]
    for at in range(2):
        for first, grad in ((at, own), (at + 2, neigh)):
            grad[:, at * lanes : (at + 1) * lanes] = (
                source[first * height : (first + 1) * height, :].astype(jnp.float32) * factor
            )


def output_body(came, held, degree, features, self_weight, neigh_weight, out):
    sums = came[...].astype(jnp.float32) + held[...]
    aggregate = (sums / column(degree, out.shape[1])).astype(jnp.bfloat16)
    out[...] = (
        dot(features[...], self_weight[...], 1, 0) + dot(aggregate, neigh_weight[...], 1, 0)
    ).astype(jnp.bfloat16)


def feature_body(low, high, mid, cotangent, self_weight, out):
    spread = mid[...] + low[...].astype(jnp.float32) + high[...].astype(jnp.float32)
    out[...] = (dot(cotangent[...], self_weight[...], 1, 1) + spread).astype(jnp.bfloat16)


def passed_along(value, steps):
    count = lax.axis_size(ROW)
    leading, last = max(0, -steps), min(count, count - steps)
    return lax.ppermute(value, ROW, [(source, source + steps) for source in range(leading, last)])


def crossed(value, axis, flip):
    return lax.ppermute(value, axis, [(at, at ^ flip) for at in range(lax.axis_size(axis))])


def exchange(value, axes):
    return lax.all_to_all(value, axes, 0, 0, tiled=True)


def local(
    features, self_weight, neigh_weight, tiles, tile_rows, tile_bands, tile_count, degree, cotangent
):
    ncol = lax.axis_size("y")
    near, far = lax.axis_size(NEAR), lax.axis_size("z")
    blk, width = features.shape
    lanes = width // 2
    slots = tiles.shape[2]
    tile_set = tiles[0, 0]
    rows, bands, count = tile_rows[0, 0], tile_bands[0, 0], tile_count[0]
    core, at_col = lax.axis_index("core"), lax.axis_index("y")
    spot = jnp.stack([core, at_col % 2, at_col // 2 % 2, at_col // 4]).astype(jnp.int32)
    degree = degree[None, :]
    factor = 1.0 / math.sqrt(lax.axis_size(ROW) * ncol * blk)

    below, above = passed_along(features, 2), passed_along(features, -2)
    copies = call(share_body, half(ncol * blk, width), [VM] * 2)(degree, cotangent)
    shares = exchange(copies, "y")
    pair = call(pair_body, half(2 * blk, width), [SM] + [VM] * 3)(spot, features, below, above)
    pair = crossed(pair, "core", 1)
    landing, far0, near_landed, own, far1 = call(
        backward_body,
        [half(WIDE, blk, width), half(blk, width), half(2 * blk, width)] + [half(blk, width)] * 2,
        [SM] * 3 + [VM] * 3,
        scratch=[pltpu.VMEM((WIDE + 1, blk, width), jnp.float32)],
        cost=cost(5 * 10**9, tile_set.size * 2 + 13 * features.size * 2),
    )(rows, bands, count, tile_set, shares, neigh_weight)

    grads, window = call(
        grads_body,
        [half(4 * width, lanes), half(WIDE, blk, width)],
        [SM] + [VM] * 6,
        cost=cost(2 * (WIDE + 1) * blk * width * width, 18 * features.size * 2),
    )(spot, cotangent, below, pair, features, above, landing)
    scattered = exchange(grads, NEAR)

    sent, kept = call(
        forward_body,
        [half(ncol // 2 * blk, width)] * 2,
        [SM] * 4 + [VM] * 2 + [HB],
        scratch=[pltpu.VMEM((ncol + 1, blk, width), jnp.float32)],
        cost=cost(5 * 10**9, tile_set.size * 2 + 13 * features.size * 2),
    )(rows, bands, count, spot, tile_set, window, grads)
    came = crossed(sent, "y", 1)
    near_landed = crossed(near_landed, "core", 1)
    sent, kept = call(
        halve_body(blk, 2),
        [half(ncol // 4 * blk, width), full(ncol // 4 * blk, width)],
        [SM] + [VM] * 2,
    )(spot, came, kept)
    low, high, mid = call(
        merge_body, [half(blk, width)] * 2 + [full(blk, width)], [SM] + [VM] * 4
    )(spot, near_landed, far0, far1, own)

    joined = fold_spread(scattered, near, far, after=[low])
    joined = exchange(joined, "z")

    came = crossed(sent, "y", 2)
    low, high = passed_along(low, -2), passed_along(high, 2)
    grads = fold_spread(joined, far, near, after=[sent])
    gathered = exchange(grads, NEAR)

    sent, kept = call(
        halve_body(blk, 3),
        [half(blk, width), full(blk, width)],
        [SM] + [VM] * 2 + [HB],
        cost=cost(2 * 10**9, 0),
    )(spot, came, kept, grads)
    feature_grad = call(feature_body, half(blk, width), [VM] * 5, cost=cost(4 * 10**9, 0))(
        low, high, mid, cotangent, self_weight
    )
    came = crossed(sent, "y", 4)
    output = call(output_body, half(blk, width), [VM] * 6, cost=cost(2 * 10**9, 0))(
        came, kept, degree, features, self_weight, neigh_weight
    )
    self_grad, neigh_grad = call(
        functools.partial(finish_body, factor), [full(width, width)] * 2, [VM]
    )(gathered)
    return (output, feature_grad, self_grad, neigh_grad)


def solution(mesh):
    fine = Mesh(
        np.array(mesh.devices).reshape(mesh.shape["row"] // 8, 4, 2, mesh.shape["col"]),
        ROW + ("y",),
    )
    nodes = ROW + ("y",)
    in_specs = (
        P(nodes, None),
        P(),
        P(),
        P(ROW, "y", None, None, None),
        P(ROW, "y", None),
        P(ROW, "y", None),
        P(ROW, "y"),
        P(nodes),
        P(nodes, None),
    )
    out_specs = (P(nodes, None), P(nodes, None), P(), P())
    return jax.shard_map(local, mesh=fine, in_specs=in_specs, out_specs=out_specs, check_vma=False)
```

```python
import functools
import math

import jax
import jax.numpy as jnp
import numpy as np
from jax import lax
from jax.experimental import pallas as pl
from jax.experimental.pallas import tpu as pltpu
from jax.sharding import Mesh
from jax.sharding import PartitionSpec as P

HALO = 2
WIDE = 2 * HALO + 1
ROW = ("z", "x", "core")
NEAR = ("x", "core", "y")
LIMIT = 48 * 1024 * 1024

VM = pl.BlockSpec(memory_space=pltpu.VMEM)
SM = pl.BlockSpec(memory_space=pltpu.SMEM)
HB = pl.BlockSpec(memory_space=pl.ANY)


def call(body, outs, in_specs, scratch=(), cost=None, out_specs=None, aliases=None):
    return pl.pallas_call(
        body,
        out_shape=outs,
        in_specs=in_specs,
        out_specs=out_specs or ([VM] * len(outs) if isinstance(outs, list) else VM),
        scratch_shapes=list(scratch),
        cost_estimate=cost,
        input_output_aliases=aliases or {},
        compiler_params=pltpu.CompilerParams(vmem_limit_bytes=LIMIT),
    )


def half(*shape):
    return jax.ShapeDtypeStruct(shape, jnp.bfloat16)


def full(*shape):
    return jax.ShapeDtypeStruct(shape, jnp.float32)


def dot(a, b, ca, cb):
    return lax.dot_general(a, b, (((ca,), (cb,)), ((), ())), preferred_element_type=jnp.float32)


def cost(flops, moved):
    return pl.CostEstimate(flops=flops, bytes_accessed=moved, transcendentals=0)


def pair_body(spot, rows, bands, own, below, above, out):
    blk = own.shape[0]
    out[:blk, :] = own[...]
    out[blk:, :] = jnp.where(spot[0] == 0, above[...], below[...])


def forward_body(
    rows, bands, count, spot, tiles, f0, pair, own, f4, out, sent, kept, window, total
):
    slots, blk = tiles.shape[0], tiles.shape[1]
    ncol = total.shape[0] - 1
    core, bit = spot[0], spot[1]
    window[0] = f0[...]
    window[1 + 2 * (1 - core)] = pair[:blk, :]
    window[2] = own[...]
    window[1 + 2 * core] = pair[blk:, :]
    window[4] = f4[...]
    total[...] = jnp.zeros_like(total)
    for slot in range(slots):
        place = jnp.where(slot < count[0], rows[slot], ncol)
        total[place] += dot(tiles[slot], window[bands[slot]], 1, 0)
    for at in range(ncol):
        out[at * blk : (at + 1) * blk, :] = total[at].astype(jnp.bfloat16)
    for at in range(ncol // 2):
        sent[at * blk : (at + 1) * blk, :] = total[2 * at + 1 - bit].astype(jnp.bfloat16)
        kept[at * blk : (at + 1) * blk, :] = total[2 * at + bit].astype(jnp.bfloat16)


def halve_body(blk, which):
    def body(spot, came, held, *rest):
        sent, kept = rest[-2:]
        rows = sent.shape[0]
        for out, side in ((sent, 1 - spot[which]), (kept, spot[which])):
            part = pl.ds(pl.multiple_of(side * rows, blk), rows)
            total = came[part, :].astype(jnp.float32) + held[part, :].astype(jnp.float32)
            out[...] = total.astype(out.dtype)

    return body


def column(degree, width):
    blk = degree.shape[1]
    tall = jnp.broadcast_to(degree[...].astype(jnp.float32), (blk, blk)).T
    return jnp.concatenate([tall] * (width // blk), axis=1)


def share_body(degree, cotangent, out, norm, block, share, sems):
    blk, width = block.shape
    first = pltpu.make_async_copy(degree, norm, sems.at[0])
    second = pltpu.make_async_copy(cotangent, block, sems.at[1])
    first.start()
    second.start()
    first.wait()
    second.wait()
    share[...] = (block[...].astype(jnp.float32) / column(norm, width)).astype(jnp.bfloat16)
    copies = [
        pltpu.make_async_copy(share, out.at[pl.ds(at * blk, blk), :], sems.at[2 + at])
        for at in range(out.shape[0] // blk)
    ]
    for copy in copies:
        copy.start()
    for copy in copies:
        copy.wait()


def grads_body(features, cotangent, partial, shares, sent, out, passed):
    own = dot(features[...], cotangent[...], 0, 0).astype(jnp.bfloat16)
    neigh = dot(partial[...], shares[...], 0, 0).astype(jnp.bfloat16)
    height, lanes = own.shape[0], out.shape[1]
    for at in range(2):
        out[at * height : (at + 1) * height, :] = own[:, at * lanes : (at + 1) * lanes]
        out[(at + 2) * height : (at + 3) * height, :] = neigh[:, at * lanes : (at + 1) * lanes]


def backward_body(rows, bands, count, tiles, shares, weight, after, far0, near, own, far1, total):
    slots, blk = tiles.shape[0], tiles.shape[1]
    total[...] = jnp.zeros_like(total)
    for slot in range(slots):
        place = jnp.where(slot < count[0], bands[slot], WIDE)
        start = pl.multiple_of(rows[slot] * blk, blk)
        total[place] += dot(tiles[slot], shares[pl.ds(start, blk), :], 0, 0)
    landed = [
        dot(total[at].astype(jnp.bfloat16), weight[...], 1, 1).astype(jnp.bfloat16)
        for at in range(WIDE)
    ]
    far0[...], own[...], far1[...] = landed[0], landed[2], landed[4]
    near[:blk, :], near[blk:, :] = landed[1], landed[3]


def merge_body(spot, came, far0, far1, own, low, high, mid):
    blk = own.shape[0]
    core = spot[0]
    lower = came[:blk, :].astype(jnp.float32)
    upper = came[blk:, :].astype(jnp.float32)
    low[...] = jnp.where(core == 1, far0[...].astype(jnp.float32) + lower, far0[...].astype(jnp.float32)).astype(low.dtype)
    high[...] = jnp.where(core == 0, far1[...].astype(jnp.float32) + upper, far1[...].astype(jnp.float32)).astype(high.dtype)
    mid[...] = own[...].astype(jnp.float32) + jnp.where(core == 0, lower, upper)


def fold(source, members):
    rows = source.shape[0] // members
    total = source[:rows, :].astype(jnp.float32)
    for at in range(1, members):
        total = total + source[at * rows : (at + 1) * rows, :].astype(jnp.float32)
    return total


def fold_spread(value, members, copies, after=()):
    rows, lanes = value.shape[0] // members, value.shape[1]

    def body(*refs):
        total = fold(refs[0], members).astype(jnp.bfloat16)
        for at in range(copies):
            refs[-1][at * rows : (at + 1) * rows, :] = total

    return call(body, half(copies * rows, lanes), [VM] + [HB] * len(after))(value, *after)


def finish_body(factor, source, own, neigh):
    height, lanes = own.shape[0], source.shape[1]
    for at in range(2):
        for first, grad in ((at, own), (at + 2, neigh)):
            grad[:, at * lanes : (at + 1) * lanes] = (
                source[first * height : (first + 1) * height, :].astype(jnp.float32) * factor
            )


def output_body(came, held, degree, features, self_weight, neigh_weight, out):
    sums = came[...].astype(jnp.float32) + held[...]
    aggregate = (sums / column(degree, out.shape[1])).astype(jnp.bfloat16)
    out[...] = (
        dot(features[...], self_weight[...], 1, 0) + dot(aggregate, neigh_weight[...], 1, 0)
    ).astype(jnp.bfloat16)


def feature_body(low, high, mid, cotangent, self_weight, out):
    spread = mid[...] + low[...].astype(jnp.float32) + high[...].astype(jnp.float32)
    out[...] = (dot(cotangent[...], self_weight[...], 1, 1) + spread).astype(jnp.bfloat16)


def passed_along(value, steps):
    count = lax.axis_size(ROW)
    leading, last = max(0, -steps), min(count, count - steps)
    return lax.ppermute(value, ROW, [(source, source + steps) for source in range(leading, last)])


def crossed(value, axis, flip):
    return lax.ppermute(value, axis, [(at, at ^ flip) for at in range(lax.axis_size(axis))])


def exchange(value, axes):
    return lax.all_to_all(value, axes, 0, 0, tiled=True)


def local(
    features, self_weight, neigh_weight, tiles, tile_rows, tile_bands, tile_count, degree, cotangent
):
    ncol = lax.axis_size("y")
    near, far = lax.axis_size(NEAR), lax.axis_size("z")
    blk, width = features.shape
    lanes = width // 2
    slots = tiles.shape[2]
    tile_set = tiles[0, 0]
    rows, bands, count = tile_rows[0, 0], tile_bands[0, 0], tile_count[0]
    core, at_col = lax.axis_index("core"), lax.axis_index("y")
    spot = jnp.stack([core, at_col & 1, at_col >> 2, (at_col >> 1) & 1]).astype(jnp.int32)
    degree = degree[None, :]
    factor = 1.0 / math.sqrt(lax.axis_size(ROW) * ncol * blk)

    below, above = passed_along(features, 2), passed_along(features, -2)
    copies = call(
        share_body,
        half(ncol * blk, width),
        [HB] * 2,
        scratch=[
            pltpu.VMEM((1, blk), jnp.int32),
            pltpu.VMEM((blk, width), jnp.bfloat16),
            pltpu.VMEM((blk, width), jnp.bfloat16),
            pltpu.SemaphoreType.DMA((2 + ncol,)),
        ],
        out_specs=HB,
    )(*(pltpu.with_memory_space_constraint(item, pltpu.HBM) for item in (degree, cotangent)))
    shares = exchange(copies, "y")
    pair = call(pair_body, half(2 * blk, width), [SM] * 3 + [VM] * 3)(
        spot, rows, bands, features, below, above
    )
    pair = crossed(pair, "core", 1)
    partial, sent, kept = call(
        forward_body,
        [half(ncol * blk, width)] + [half(ncol // 2 * blk, width)] * 2,
        [SM] * 4 + [VM] * 5,
        scratch=[
            pltpu.VMEM((WIDE, blk, width), jnp.bfloat16),
            pltpu.VMEM((ncol + 1, blk, width), jnp.float32),
        ],
        cost=cost(4 * 10**9, tile_set.size * 2 + 21 * features.size * 2),
    )(rows, bands, count, spot, tile_set, below, pair, features, above)

    grads, sent = call(
        grads_body,
        [half(4 * width, lanes), half(*sent.shape)],
        [VM] * 4 + [HB],
        out_specs=[VM, HB],
        aliases={4: 1},
        cost=cost(2 * (ncol + 1) * blk * width * width, 18 * features.size * 2),
    )(features, cotangent, partial, shares, sent)
    scattered = exchange(grads, NEAR)
    came = crossed(sent, "y", 1)

    far0, near_landed, own, far1 = call(
        backward_body,
        [half(blk, width), half(2 * blk, width), half(blk, width), half(blk, width)],
        [SM] * 3 + [VM] * 3 + [HB],
        scratch=[pltpu.VMEM((WIDE + 1, blk, width), jnp.float32)],
        cost=cost(5 * 10**9, tile_set.size * 2 + 13 * features.size * 2),
    )(rows, bands, count, tile_set, shares, neigh_weight, grads)
    near_landed = crossed(near_landed, "core", 1)
    sent, kept = call(
        halve_body(blk, 2),
        [half(ncol // 4 * blk, width), full(ncol // 4 * blk, width)],
        [SM] + [VM] * 2,
    )(spot, came, kept)
    low, high, mid = call(
        merge_body, [half(blk, width)] * 2 + [full(blk, width)], [SM] + [VM] * 4
    )(spot, near_landed, far0, far1, own)

    joined = fold_spread(scattered, near, far, after=[low])
    joined = exchange(joined, "z")

    came = crossed(sent, "y", 4)
    low, high = passed_along(low, -2), passed_along(high, 2)
    grads = fold_spread(joined, far, near, after=[sent])
    gathered = exchange(grads, NEAR)

    sent, kept = call(
        halve_body(blk, 3),
        [half(blk, width), full(blk, width)],
        [SM] + [VM] * 2 + [HB],
        cost=cost(2 * 10**9, 0),
    )(spot, came, kept, grads)
    feature_grad = call(feature_body, half(blk, width), [VM] * 5, cost=cost(4 * 10**9, 0))(
        low, high, mid, cotangent, self_weight
    )
    came = crossed(sent, "y", 2)
    output = call(output_body, half(blk, width), [VM] * 6, cost=cost(2 * 10**9, 0))(
        came, kept, degree, features, self_weight, neigh_weight
    )
    self_grad, neigh_grad = call(
        functools.partial(finish_body, factor), [full(width, width)] * 2, [VM]
    )(gathered)
    return (output, feature_grad, self_grad, neigh_grad)


def solution(mesh):
    fine = Mesh(
        np.array(mesh.devices).reshape(mesh.shape["row"] // 8, 4, 2, mesh.shape["col"]),
        ROW + ("y",),
    )
    nodes = ROW + ("y",)
    in_specs = (
        P(nodes, None),
        P(),
        P(),
        P(ROW, "y", None, None, None),
        P(ROW, "y", None),
        P(ROW, "y", None),
        P(ROW, "y"),
        P(nodes),
        P(nodes, None),
    )
    out_specs = (P(nodes, None), P(nodes, None), P(), P())
    return jax.shard_map(local, mesh=fine, in_specs=in_specs, out_specs=out_specs, check_vma=False)
```

```python
import functools
import math

import jax
import jax.numpy as jnp
import numpy as np
from jax import lax
from jax.experimental import pallas as pl
from jax.experimental.pallas import tpu as pltpu
from jax.sharding import Mesh
from jax.sharding import PartitionSpec as P

HALO = 2
WIDE = 2 * HALO + 1
ROW = ("z", "x", "core")
NEAR = ("x", "core", "y")
LIMIT = 48 * 1024 * 1024

VM = pl.BlockSpec(memory_space=pltpu.VMEM)
SM = pl.BlockSpec(memory_space=pltpu.SMEM)
HB = pl.BlockSpec(memory_space=pl.ANY)


def call(body, outs, in_specs, scratch=(), cost=None, out_specs=None, aliases=None):
    return pl.pallas_call(
        body,
        out_shape=outs,
        in_specs=in_specs,
        out_specs=out_specs or ([VM] * len(outs) if isinstance(outs, list) else VM),
        scratch_shapes=list(scratch),
        cost_estimate=cost,
        input_output_aliases=aliases or {},
        compiler_params=pltpu.CompilerParams(vmem_limit_bytes=LIMIT),
    )


def half(*shape):
    return jax.ShapeDtypeStruct(shape, jnp.bfloat16)


def full(*shape):
    return jax.ShapeDtypeStruct(shape, jnp.float32)


def dot(a, b, ca, cb):
    return lax.dot_general(a, b, (((ca,), (cb,)), ((), ())), preferred_element_type=jnp.float32)


def cost(flops, moved):
    return pl.CostEstimate(flops=flops, bytes_accessed=moved, transcendentals=0)


def pair_body(spot, own, below, above, out):
    blk = own.shape[0]
    out[:blk, :] = own[...]
    out[blk:, :] = jnp.where(spot[0] == 0, above[...], below[...])


def forward_body(
    rows, bands, count, spot, tiles, f0, pair, own, f4, out, sent, kept, window, total
):
    slots, blk = tiles.shape[0], tiles.shape[1]
    ncol = total.shape[0] - 1
    core, bit = spot[0], spot[1]
    window[0] = f0[...]
    window[1 + 2 * (1 - core)] = pair[:blk, :]
    window[2] = own[...]
    window[1 + 2 * core] = pair[blk:, :]
    window[4] = f4[...]
    total[...] = jnp.zeros_like(total)
    for slot in range(slots):
        place = jnp.where(slot < count[0], rows[slot], ncol)
        total[place] += dot(tiles[slot], window[bands[slot]], 1, 0)
    for at in range(ncol):
        out[at * blk : (at + 1) * blk, :] = total[at].astype(jnp.bfloat16)
    for at in range(ncol // 2):
        sent[at * blk : (at + 1) * blk, :] = total[2 * at + 1 - bit].astype(jnp.bfloat16)
        kept[at * blk : (at + 1) * blk, :] = total[2 * at + bit].astype(jnp.bfloat16)


def halve_body(blk, which):
    def body(spot, came, held, *rest):
        sent, kept = rest[-2:]
        rows = sent.shape[0]
        for out, side in ((sent, 1 - spot[which]), (kept, spot[which])):
            part = pl.ds(pl.multiple_of(side * rows, blk), rows)
            total = came[part, :].astype(jnp.float32) + held[part, :].astype(jnp.float32)
            out[...] = total.astype(out.dtype)

    return body


def column(degree, width):
    blk = degree.shape[1]
    tall = jnp.broadcast_to(degree[...].astype(jnp.float32), (blk, blk)).T
    return jnp.concatenate([tall] * (width // blk), axis=1)


def share_body(degree, cotangent, rows, bands, out, rows_out, bands_out, norm, block, share, sems):
    blk, width = block.shape
    first = pltpu.make_async_copy(degree, norm, sems.at[0])
    second = pltpu.make_async_copy(cotangent, block, sems.at[1])
    first.start()
    second.start()
    ncol = out.shape[0] // blk
    tables = [
        pltpu.make_async_copy(rows, rows_out, sems.at[2 + ncol]),
        pltpu.make_async_copy(bands, bands_out, sems.at[3 + ncol]),
    ]
    for table in tables:
        table.start()
    first.wait()
    second.wait()
    share[...] = (block[...].astype(jnp.float32) / column(norm, width)).astype(jnp.bfloat16)
    copies = [
        pltpu.make_async_copy(share, out.at[pl.ds(at * blk, blk), :], sems.at[2 + at])
        for at in range(ncol)
    ]
    for copy in copies:
        copy.start()
    for copy in tables + copies:
        copy.wait()


def grads_body(features, cotangent, partial, shares, out):
    own = dot(features[...], cotangent[...], 0, 0).astype(jnp.bfloat16)
    neigh = dot(partial[...], shares[...], 0, 0).astype(jnp.bfloat16)
    height, lanes = own.shape[0], out.shape[1]
    for at in range(2):
        out[at * height : (at + 1) * height, :] = own[:, at * lanes : (at + 1) * lanes]
        out[(at + 2) * height : (at + 3) * height, :] = neigh[:, at * lanes : (at + 1) * lanes]


def backward_body(
    rows, bands, count, tiles, shares, weight, after, sent, far0, near, own, far1, passed, total
):
    slots, blk = tiles.shape[0], tiles.shape[1]
    total[...] = jnp.zeros_like(total)
    for slot in range(slots):
        place = jnp.where(slot < count[0], bands[slot], WIDE)
        start = pl.multiple_of(rows[slot] * blk, blk)
        total[place] += dot(tiles[slot], shares[pl.ds(start, blk), :], 0, 0)
    landed = [
        dot(total[at].astype(jnp.bfloat16), weight[...], 1, 1).astype(jnp.bfloat16)
        for at in range(WIDE)
    ]
    far0[...], own[...], far1[...] = landed[0], landed[2], landed[4]
    near[:blk, :], near[blk:, :] = landed[1], landed[3]


def merge_body(spot, came, far0, far1, own, low, high, mid):
    blk = own.shape[0]
    core = spot[0]
    lower = came[:blk, :].astype(jnp.float32)
    upper = came[blk:, :].astype(jnp.float32)
    low[...] = jnp.where(core == 1, far0[...].astype(jnp.float32) + lower, far0[...].astype(jnp.float32)).astype(low.dtype)
    high[...] = jnp.where(core == 0, far1[...].astype(jnp.float32) + upper, far1[...].astype(jnp.float32)).astype(high.dtype)
    mid[...] = own[...].astype(jnp.float32) + jnp.where(core == 0, lower, upper)


def fold(source, members):
    rows = source.shape[0] // members
    total = source[:rows, :].astype(jnp.float32)
    for at in range(1, members):
        total = total + source[at * rows : (at + 1) * rows, :].astype(jnp.float32)
    return total


def fold_spread(value, members, copies, after=()):
    rows, lanes = value.shape[0] // members, value.shape[1]

    def body(*refs):
        total = fold(refs[0], members).astype(jnp.bfloat16)
        for at in range(copies):
            refs[-1][at * rows : (at + 1) * rows, :] = total

    return call(body, half(copies * rows, lanes), [VM] + [HB] * len(after))(value, *after)


def finish_body(factor, source, own, neigh):
    height, lanes = own.shape[0], source.shape[1]
    for at in range(2):
        for first, grad in ((at, own), (at + 2, neigh)):
            grad[:, at * lanes : (at + 1) * lanes] = (
                source[first * height : (first + 1) * height, :].astype(jnp.float32) * factor
            )


def output_body(came, held, degree, features, self_weight, neigh_weight, out):
    sums = came[...].astype(jnp.float32) + held[...]
    aggregate = (sums / column(degree, out.shape[1])).astype(jnp.bfloat16)
    out[...] = (
        dot(features[...], self_weight[...], 1, 0) + dot(aggregate, neigh_weight[...], 1, 0)
    ).astype(jnp.bfloat16)


def feature_body(low, high, mid, cotangent, self_weight, out):
    spread = mid[...] + low[...].astype(jnp.float32) + high[...].astype(jnp.float32)
    out[...] = (dot(cotangent[...], self_weight[...], 1, 1) + spread).astype(jnp.bfloat16)


def passed_along(value, steps):
    count = lax.axis_size(ROW)
    leading, last = max(0, -steps), min(count, count - steps)
    return lax.ppermute(value, ROW, [(source, source + steps) for source in range(leading, last)])


def crossed(value, axis, flip):
    return lax.ppermute(value, axis, [(at, at ^ flip) for at in range(lax.axis_size(axis))])


def exchange(value, axes):
    return lax.all_to_all(value, axes, 0, 0, tiled=True)


def local(
    features, self_weight, neigh_weight, tiles, tile_rows, tile_bands, tile_count, degree, cotangent
):
    ncol = lax.axis_size("y")
    near, far = lax.axis_size(NEAR), lax.axis_size("z")
    blk, width = features.shape
    lanes = width // 2
    slots = tiles.shape[2]
    tile_set = tiles[0, 0]
    rows, bands, count = tile_rows[0, 0], tile_bands[0, 0], tile_count[0]
    core, at_col = lax.axis_index("core"), lax.axis_index("y")
    spot = jnp.stack([core, at_col & 1, at_col >> 2, (at_col >> 1) & 1]).astype(jnp.int32)
    degree = degree[None, :]
    factor = 1.0 / math.sqrt(lax.axis_size(ROW) * ncol * blk)

    below, above = passed_along(features, 2), passed_along(features, -2)
    table = jax.ShapeDtypeStruct((slots,), jnp.int32)
    given = [
        pltpu.with_memory_space_constraint(item, pltpu.HBM)
        for item in (degree, cotangent, rows, bands)
    ]
    copies, rows, bands = call(
        share_body,
        [half(ncol * blk, width), table, table],
        [HB] * 4,
        scratch=[
            pltpu.VMEM((1, blk), jnp.int32),
            pltpu.VMEM((blk, width), jnp.bfloat16),
            pltpu.VMEM((blk, width), jnp.bfloat16),
            pltpu.SemaphoreType.DMA((4 + ncol,)),
        ],
        out_specs=[HB, VM, VM],
    )(*given)
    shares = exchange(copies, "y")
    pair = call(pair_body, half(2 * blk, width), [SM] + [VM] * 3)(spot, features, below, above)
    pair = crossed(pair, "core", 1)
    partial, sent, kept = call(
        forward_body,
        [half(ncol * blk, width)] + [half(ncol // 2 * blk, width)] * 2,
        [SM] * 4 + [VM] * 5,
        scratch=[
            pltpu.VMEM((WIDE, blk, width), jnp.bfloat16),
            pltpu.VMEM((ncol + 1, blk, width), jnp.float32),
        ],
        cost=cost(4 * 10**9, tile_set.size * 2 + 21 * features.size * 2),
    )(rows, bands, count, spot, tile_set, below, pair, features, above)

    grads = call(
        grads_body,
        half(4 * width, lanes),
        [VM] * 4,
        cost=cost(2 * (ncol + 1) * blk * width * width, 18 * features.size * 2),
    )(features, cotangent, partial, shares)
    scattered = exchange(grads, NEAR)

    far0, near_landed, own, far1, sent = call(
        backward_body,
        [half(blk, width), half(2 * blk, width), half(blk, width), half(blk, width)]
        + [half(*sent.shape)],
        [SM] * 3 + [VM] * 3 + [HB] * 2,
        out_specs=[VM] * 4 + [HB],
        aliases={7: 4},
        scratch=[pltpu.VMEM((WIDE + 1, blk, width), jnp.float32)],
        cost=cost(5 * 10**9, tile_set.size * 2 + 13 * features.size * 2),
    )(rows, bands, count, tile_set, shares, neigh_weight, grads, sent)
    came = crossed(sent, "y", 1)
    near_landed = crossed(near_landed, "core", 1)
    sent, kept = call(
        halve_body(blk, 2),
        [half(ncol // 4 * blk, width), full(ncol // 4 * blk, width)],
        [SM] + [VM] * 2,
    )(spot, came, kept)
    low, high, mid = call(
        merge_body, [half(blk, width)] * 2 + [full(blk, width)], [SM] + [VM] * 4
    )(spot, near_landed, far0, far1, own)

    joined = fold_spread(scattered, near, far, after=[low])
    joined = exchange(joined, "z")

    came = crossed(sent, "y", 4)
    low, high = passed_along(low, -2), passed_along(high, 2)
    grads = fold_spread(joined, far, near, after=[sent])
    gathered = exchange(grads, NEAR)

    sent, kept = call(
        halve_body(blk, 3),
        [half(blk, width), full(blk, width)],
        [SM] + [VM] * 2 + [HB],
        cost=cost(2 * 10**9, 0),
    )(spot, came, kept, grads)
    feature_grad = call(feature_body, half(blk, width), [VM] * 5, cost=cost(4 * 10**9, 0))(
        low, high, mid, cotangent, self_weight
    )
    came = crossed(sent, "y", 2)
    output = call(output_body, half(blk, width), [VM] * 6, cost=cost(2 * 10**9, 0))(
        came, kept, degree, features, self_weight, neigh_weight
    )
    self_grad, neigh_grad = call(
        functools.partial(finish_body, factor), [full(width, width)] * 2, [VM]
    )(gathered)
    return (output, feature_grad, self_grad, neigh_grad)


def solution(mesh):
    fine = Mesh(
        np.array(mesh.devices).reshape(mesh.shape["row"] // 8, 4, 2, mesh.shape["col"]),
        ROW + ("y",),
    )
    nodes = ROW + ("y",)
    in_specs = (
        P(nodes, None),
        P(),
        P(),
        P(ROW, "y", None, None, None),
        P(ROW, "y", None),
        P(ROW, "y", None),
        P(ROW, "y"),
        P(nodes),
        P(nodes, None),
    )
    out_specs = (P(nodes, None), P(nodes, None), P(), P())
    return jax.shard_map(local, mesh=fine, in_specs=in_specs, out_specs=out_specs, check_vma=False)
```

```python
import functools
import math

import jax
import jax.numpy as jnp
import numpy as np
from jax import lax
from jax.experimental import pallas as pl
from jax.experimental.pallas import tpu as pltpu
from jax.sharding import Mesh
from jax.sharding import PartitionSpec as P

HALO = 2
WIDE = 2 * HALO + 1
ROW = ("z", "x", "core")
NEAR = ("x", "core", "y")
LIMIT = 48 * 1024 * 1024

VM = pl.BlockSpec(memory_space=pltpu.VMEM)
SM = pl.BlockSpec(memory_space=pltpu.SMEM)
HB = pl.BlockSpec(memory_space=pl.ANY)


def call(body, outs, in_specs, scratch=(), cost=None, out_specs=None, aliases=None):
    return pl.pallas_call(
        body,
        out_shape=outs,
        in_specs=in_specs,
        out_specs=out_specs or ([VM] * len(outs) if isinstance(outs, list) else VM),
        scratch_shapes=list(scratch),
        cost_estimate=cost,
        input_output_aliases=aliases or {},
        compiler_params=pltpu.CompilerParams(vmem_limit_bytes=LIMIT),
    )


def half(*shape):
    return jax.ShapeDtypeStruct(shape, jnp.bfloat16)


def full(*shape):
    return jax.ShapeDtypeStruct(shape, jnp.float32)


def dot(a, b, ca, cb):
    return lax.dot_general(a, b, (((ca,), (cb,)), ((), ())), preferred_element_type=jnp.float32)


def cost(flops, moved):
    return pl.CostEstimate(flops=flops, bytes_accessed=moved, transcendentals=0)


def pair_body(spot, own, below, above, out):
    blk = own.shape[0]
    out[:blk, :] = own[...]
    out[blk:, :] = jnp.where(spot[0] == 0, above[...], below[...])


def forward_body(
    rows, bands, count, spot, tiles, f0, pair, own, f4, out, sent, kept, window, total
):
    slots, blk = tiles.shape[0], tiles.shape[1]
    ncol = total.shape[0] - 1
    core, bit = spot[0], spot[1]
    window[0] = f0[...]
    window[1 + 2 * (1 - core)] = pair[:blk, :]
    window[2] = own[...]
    window[1 + 2 * core] = pair[blk:, :]
    window[4] = f4[...]
    total[...] = jnp.zeros_like(total)
    for slot in range(slots):
        place = jnp.where(slot < count[0], rows[slot], ncol)
        total[place] += dot(tiles[slot], window[bands[slot]], 1, 0)
    for at in range(ncol):
        out[at * blk : (at + 1) * blk, :] = total[at].astype(jnp.bfloat16)
    for at in range(ncol // 2):
        sent[at * blk : (at + 1) * blk, :] = total[2 * at + 1 - bit].astype(jnp.bfloat16)
        kept[at * blk : (at + 1) * blk, :] = total[2 * at + bit].astype(jnp.bfloat16)


def halve_body(blk, which):
    def body(spot, came, held, *rest):
        sent, kept = rest[-2:]
        rows = sent.shape[0]
        for out, side in ((sent, 1 - spot[which]), (kept, spot[which])):
            part = pl.ds(pl.multiple_of(side * rows, blk), rows)
            total = came[part, :].astype(jnp.float32) + held[part, :].astype(jnp.float32)
            out[...] = total.astype(out.dtype)

    return body


def column(degree, width):
    blk = degree.shape[1]
    tall = jnp.broadcast_to(degree[...].astype(jnp.float32), (blk, blk)).T
    return jnp.concatenate([tall] * (width // blk), axis=1)


def share_body(degree, cotangent, rows, bands, out, rows_out, bands_out, norm, block, share, sems):
    blk, width = block.shape
    first = pltpu.make_async_copy(degree, norm, sems.at[0])
    second = pltpu.make_async_copy(cotangent, block, sems.at[1])
    first.start()
    second.start()
    ncol = out.shape[0] // blk
    tables = [
        pltpu.make_async_copy(rows, rows_out, sems.at[2 + ncol]),
        pltpu.make_async_copy(bands, bands_out, sems.at[3 + ncol]),
    ]
    for table in tables:
        table.start()
    first.wait()
    second.wait()
    share[...] = (block[...].astype(jnp.float32) / column(norm, width)).astype(jnp.bfloat16)
    copies = [
        pltpu.make_async_copy(share, out.at[pl.ds(at * blk, blk), :], sems.at[2 + at])
        for at in range(ncol)
    ]
    for copy in copies:
        copy.start()
    for copy in tables + copies:
        copy.wait()


def grads_body(features, cotangent, partial, shares, out):
    own = dot(features[...], cotangent[...], 0, 0).astype(jnp.bfloat16)
    neigh = dot(partial[...], shares[...], 0, 0).astype(jnp.bfloat16)
    height, lanes = own.shape[0], out.shape[1]
    for at in range(2):
        out[at * height : (at + 1) * height, :] = own[:, at * lanes : (at + 1) * lanes]
        out[(at + 2) * height : (at + 3) * height, :] = neigh[:, at * lanes : (at + 1) * lanes]


def backward_body(
    rows, bands, count, tiles, shares, weight, after, sent, far0, near, own, far1, passed, total
):
    slots, blk = tiles.shape[0], tiles.shape[1]
    total[...] = jnp.zeros_like(total)
    for slot in range(slots):
        place = jnp.where(slot < count[0], bands[slot], WIDE)
        start = pl.multiple_of(rows[slot] * blk, blk)
        total[place] += dot(tiles[slot], shares[pl.ds(start, blk), :], 0, 0)
    landed = [
        dot(total[at].astype(jnp.bfloat16), weight[...], 1, 1).astype(jnp.bfloat16)
        for at in range(WIDE)
    ]
    far0[...], own[...], far1[...] = landed[0], landed[2], landed[4]
    near[:blk, :], near[blk:, :] = landed[1], landed[3]


def merge_body(spot, came, far0, far1, own, low, high, mid):
    blk = own.shape[0]
    core = spot[0]
    lower = came[:blk, :].astype(jnp.float32)
    upper = came[blk:, :].astype(jnp.float32)
    low[...] = jnp.where(core == 1, far0[...].astype(jnp.float32) + lower, far0[...].astype(jnp.float32)).astype(low.dtype)
    high[...] = jnp.where(core == 0, far1[...].astype(jnp.float32) + upper, far1[...].astype(jnp.float32)).astype(high.dtype)
    mid[...] = own[...].astype(jnp.float32) + jnp.where(core == 0, lower, upper)


def fold(source, members):
    rows = source.shape[0] // members
    total = source[:rows, :].astype(jnp.float32)
    for at in range(1, members):
        total = total + source[at * rows : (at + 1) * rows, :].astype(jnp.float32)
    return total


def fold_spread(value, members, copies, after=(), weight=0):
    rows, lanes = value.shape[0] // members, value.shape[1]

    def body(*refs):
        total = fold(refs[0], members).astype(jnp.bfloat16)
        for at in range(copies):
            refs[-1][at * rows : (at + 1) * rows, :] = total

    return call(
        body, half(copies * rows, lanes), [VM] + [HB] * len(after), cost=cost(weight, 0)
    )(value, *after)


def finish_body(factor, source, own, neigh):
    height, lanes = own.shape[0], source.shape[1]
    for at in range(2):
        for first, grad in ((at, own), (at + 2, neigh)):
            grad[:, at * lanes : (at + 1) * lanes] = (
                source[first * height : (first + 1) * height, :].astype(jnp.float32) * factor
            )


def output_body(came, held, degree, features, self_weight, neigh_weight, out):
    sums = came[...].astype(jnp.float32) + held[...]
    aggregate = (sums / column(degree, out.shape[1])).astype(jnp.bfloat16)
    out[...] = (
        dot(features[...], self_weight[...], 1, 0) + dot(aggregate, neigh_weight[...], 1, 0)
    ).astype(jnp.bfloat16)


def feature_body(low, high, mid, cotangent, self_weight, out):
    spread = mid[...] + low[...].astype(jnp.float32) + high[...].astype(jnp.float32)
    out[...] = (dot(cotangent[...], self_weight[...], 1, 1) + spread).astype(jnp.bfloat16)


def passed_along(value, steps):
    count = lax.axis_size(ROW)
    leading, last = max(0, -steps), min(count, count - steps)
    return lax.ppermute(value, ROW, [(source, source + steps) for source in range(leading, last)])


def crossed(value, axis, flip):
    return lax.ppermute(value, axis, [(at, at ^ flip) for at in range(lax.axis_size(axis))])


def exchange(value, axes):
    return lax.all_to_all(value, axes, 0, 0, tiled=True)


def local(
    features, self_weight, neigh_weight, tiles, tile_rows, tile_bands, tile_count, degree, cotangent
):
    ncol = lax.axis_size("y")
    near, far = lax.axis_size(NEAR), lax.axis_size("z")
    blk, width = features.shape
    lanes = width // 2
    slots = tiles.shape[2]
    tile_set = tiles[0, 0]
    rows, bands, count = tile_rows[0, 0], tile_bands[0, 0], tile_count[0]
    core, at_col = lax.axis_index("core"), lax.axis_index("y")
    spot = jnp.stack([core, at_col & 1, at_col >> 2, (at_col >> 1) & 1]).astype(jnp.int32)
    degree = degree[None, :]
    factor = 1.0 / math.sqrt(lax.axis_size(ROW) * ncol * blk)

    below, above = passed_along(features, 2), passed_along(features, -2)
    table = jax.ShapeDtypeStruct((slots,), jnp.int32)
    given = [
        pltpu.with_memory_space_constraint(item, pltpu.HBM)
        for item in (degree, cotangent, rows, bands)
    ]
    copies, rows, bands = call(
        share_body,
        [half(ncol * blk, width), table, table],
        [HB] * 4,
        scratch=[
            pltpu.VMEM((1, blk), jnp.int32),
            pltpu.VMEM((blk, width), jnp.bfloat16),
            pltpu.VMEM((blk, width), jnp.bfloat16),
            pltpu.SemaphoreType.DMA((4 + ncol,)),
        ],
        out_specs=[HB, VM, VM],
    )(*given)
    shares = exchange(copies, "y")
    pair = call(pair_body, half(2 * blk, width), [SM] + [VM] * 3)(spot, features, below, above)
    pair = crossed(pair, "core", 1)
    partial, sent, kept = call(
        forward_body,
        [half(ncol * blk, width)] + [half(ncol // 2 * blk, width)] * 2,
        [SM] * 4 + [VM] * 5,
        scratch=[
            pltpu.VMEM((WIDE, blk, width), jnp.bfloat16),
            pltpu.VMEM((ncol + 1, blk, width), jnp.float32),
        ],
        cost=cost(4 * 10**9, tile_set.size * 2 + 21 * features.size * 2),
    )(rows, bands, count, spot, tile_set, below, pair, features, above)

    grads = call(
        grads_body,
        half(4 * width, lanes),
        [VM] * 4,
        cost=cost(2 * (ncol + 1) * blk * width * width, 18 * features.size * 2),
    )(features, cotangent, partial, shares)
    scattered = exchange(grads, NEAR)

    far0, near_landed, own, far1, sent = call(
        backward_body,
        [half(blk, width), half(2 * blk, width), half(blk, width), half(blk, width)]
        + [half(*sent.shape)],
        [SM] * 3 + [VM] * 3 + [HB] * 2,
        out_specs=[VM] * 4 + [HB],
        aliases={7: 4},
        scratch=[pltpu.VMEM((WIDE + 1, blk, width), jnp.float32)],
        cost=cost(5 * 10**9, tile_set.size * 2 + 13 * features.size * 2),
    )(rows, bands, count, tile_set, shares, neigh_weight, grads, sent)
    came = crossed(sent, "y", 1)
    near_landed = crossed(near_landed, "core", 1)
    low, high, mid = call(
        merge_body, [half(blk, width)] * 2 + [full(blk, width)], [SM] + [VM] * 4
    )(spot, near_landed, far0, far1, own)
    sent, kept = call(
        halve_body(blk, 2),
        [half(ncol // 4 * blk, width), full(ncol // 4 * blk, width)],
        [SM] + [VM] * 2 + [HB],
    )(spot, came, kept, low)

    joined = fold_spread(scattered, near, far, after=[far0], weight=5 * 10**9)
    joined = exchange(joined, "z")

    came = crossed(sent, "y", 4)
    low, high = passed_along(low, -2), passed_along(high, 2)
    grads = fold_spread(joined, far, near, after=[sent])
    gathered = exchange(grads, NEAR)

    sent, kept = call(
        halve_body(blk, 3),
        [half(blk, width), full(blk, width)],
        [SM] + [VM] * 2 + [HB],
        cost=cost(2 * 10**9, 0),
    )(spot, came, kept, grads)
    feature_grad = call(feature_body, half(blk, width), [VM] * 5, cost=cost(4 * 10**9, 0))(
        low, high, mid, cotangent, self_weight
    )
    came = crossed(sent, "y", 2)
    output = call(output_body, half(blk, width), [VM] * 6, cost=cost(2 * 10**9, 0))(
        came, kept, degree, features, self_weight, neigh_weight
    )
    self_grad, neigh_grad = call(
        functools.partial(finish_body, factor), [full(width, width)] * 2, [VM]
    )(gathered)
    return (output, feature_grad, self_grad, neigh_grad)


def solution(mesh):
    fine = Mesh(
        np.array(mesh.devices).reshape(mesh.shape["row"] // 8, 4, 2, mesh.shape["col"]),
        ROW + ("y",),
    )
    nodes = ROW + ("y",)
    in_specs = (
        P(nodes, None),
        P(),
        P(),
        P(ROW, "y", None, None, None),
        P(ROW, "y", None),
        P(ROW, "y", None),
        P(ROW, "y"),
        P(nodes),
        P(nodes, None),
    )
    out_specs = (P(nodes, None), P(nodes, None), P(), P())
    return jax.shard_map(local, mesh=fine, in_specs=in_specs, out_specs=out_specs, check_vma=False)
```

```python
import functools
import math

import jax
import jax.numpy as jnp
import numpy as np
from jax import lax
from jax.experimental import pallas as pl
from jax.experimental.pallas import tpu as pltpu
from jax.sharding import Mesh
from jax.sharding import PartitionSpec as P

HALO = 2
WIDE = 2 * HALO + 1
ROW = ("z", "x", "core")
NEAR = ("core", "x", "y")
PLANE = ("x", "y")
LIMIT = 48 * 1024 * 1024

VM = pl.BlockSpec(memory_space=pltpu.VMEM)
SM = pl.BlockSpec(memory_space=pltpu.SMEM)
HB = pl.BlockSpec(memory_space=pl.ANY)


def call(body, outs, in_specs, scratch=(), cost=None, out_specs=None, aliases=None):
    return pl.pallas_call(
        body,
        out_shape=outs,
        in_specs=in_specs,
        out_specs=out_specs or ([VM] * len(outs) if isinstance(outs, list) else VM),
        scratch_shapes=list(scratch),
        cost_estimate=cost,
        input_output_aliases=aliases or {},
        compiler_params=pltpu.CompilerParams(vmem_limit_bytes=LIMIT),
    )


def half(*shape):
    return jax.ShapeDtypeStruct(shape, jnp.bfloat16)


def full(*shape):
    return jax.ShapeDtypeStruct(shape, jnp.float32)


def dot(a, b, ca, cb):
    return lax.dot_general(a, b, (((ca,), (cb,)), ((), ())), preferred_element_type=jnp.float32)


def cost(flops, moved):
    return pl.CostEstimate(flops=flops, bytes_accessed=moved, transcendentals=0)


def pair_body(spot, own, below, above, out):
    blk = own.shape[0]
    out[:blk, :] = own[...]
    out[blk:, :] = jnp.where(spot[0] == 0, above[...], below[...])


def forward_body(
    rows, bands, count, spot, tiles, f0, pair, own, f4, out, sent, kept, window, total
):
    slots, blk = tiles.shape[0], tiles.shape[1]
    ncol = total.shape[0] - 1
    core, bit = spot[0], spot[1]
    window[0] = f0[...]
    window[1 + 2 * (1 - core)] = pair[:blk, :]
    window[2] = own[...]
    window[1 + 2 * core] = pair[blk:, :]
    window[4] = f4[...]
    total[...] = jnp.zeros_like(total)
    for slot in range(slots):
        place = jnp.where(slot < count[0], rows[slot], ncol)
        total[place] += dot(tiles[slot], window[bands[slot]], 1, 0)
    for at in range(ncol):
        out[at * blk : (at + 1) * blk, :] = total[at].astype(jnp.bfloat16)
    for at in range(ncol // 2):
        sent[at * blk : (at + 1) * blk, :] = total[2 * at + 1 - bit].astype(jnp.bfloat16)
        kept[at * blk : (at + 1) * blk, :] = total[2 * at + bit].astype(jnp.bfloat16)


def halve_body(blk, which):
    def body(spot, came, held, *rest):
        sent, kept = rest[-2:]
        rows = sent.shape[0]
        for out, side in ((sent, 1 - spot[which]), (kept, spot[which])):
            part = pl.ds(pl.multiple_of(side * rows, blk), rows)
            total = came[part, :].astype(jnp.float32) + held[part, :].astype(jnp.float32)
            out[...] = total.astype(out.dtype)

    return body


def column(degree, width):
    blk = degree.shape[1]
    tall = jnp.broadcast_to(degree[...].astype(jnp.float32), (blk, blk)).T
    return jnp.concatenate([tall] * (width // blk), axis=1)


def share_body(degree, cotangent, rows, bands, out, rows_out, bands_out, norm, block, share, sems):
    blk, width = block.shape
    first = pltpu.make_async_copy(degree, norm, sems.at[0])
    second = pltpu.make_async_copy(cotangent, block, sems.at[1])
    first.start()
    second.start()
    ncol = out.shape[0] // blk
    tables = [
        pltpu.make_async_copy(rows, rows_out, sems.at[2 + ncol]),
        pltpu.make_async_copy(bands, bands_out, sems.at[3 + ncol]),
    ]
    for table in tables:
        table.start()
    first.wait()
    second.wait()
    share[...] = (block[...].astype(jnp.float32) / column(norm, width)).astype(jnp.bfloat16)
    copies = [
        pltpu.make_async_copy(share, out.at[pl.ds(at * blk, blk), :], sems.at[2 + at])
        for at in range(ncol)
    ]
    for copy in copies:
        copy.start()
    for copy in tables + copies:
        copy.wait()


def grads_body(features, cotangent, partial, shares, out):
    own = dot(features[...], cotangent[...], 0, 0).astype(jnp.bfloat16)
    neigh = dot(partial[...], shares[...], 0, 0).astype(jnp.bfloat16)
    height, lanes = own.shape[0], out.shape[1]
    for at in range(2):
        out[at * height : (at + 1) * height, :] = own[:, at * lanes : (at + 1) * lanes]
        out[(at + 2) * height : (at + 3) * height, :] = neigh[:, at * lanes : (at + 1) * lanes]


def backward_body(
    rows, bands, count, tiles, shares, weight, after, sent, far0, near, own, far1, passed, total
):
    slots, blk = tiles.shape[0], tiles.shape[1]
    total[...] = jnp.zeros_like(total)
    for slot in range(slots):
        place = jnp.where(slot < count[0], bands[slot], WIDE)
        start = pl.multiple_of(rows[slot] * blk, blk)
        total[place] += dot(tiles[slot], shares[pl.ds(start, blk), :], 0, 0)
    landed = [
        dot(total[at].astype(jnp.bfloat16), weight[...], 1, 1).astype(jnp.bfloat16)
        for at in range(WIDE)
    ]
    far0[...], own[...], far1[...] = landed[0], landed[2], landed[4]
    near[:blk, :], near[blk:, :] = landed[1], landed[3]


def merge_body(spot, came, far0, far1, own, low, high, mid):
    blk = own.shape[0]
    core = spot[0]
    lower = came[:blk, :].astype(jnp.float32)
    upper = came[blk:, :].astype(jnp.float32)
    low[...] = jnp.where(core == 1, far0[...].astype(jnp.float32) + lower, far0[...].astype(jnp.float32)).astype(low.dtype)
    high[...] = jnp.where(core == 0, far1[...].astype(jnp.float32) + upper, far1[...].astype(jnp.float32)).astype(high.dtype)
    mid[...] = own[...].astype(jnp.float32) + jnp.where(core == 0, lower, upper)


def fold(source, members):
    rows = source.shape[0] // members
    total = source[:rows, :].astype(jnp.float32)
    for at in range(1, members):
        total = total + source[at * rows : (at + 1) * rows, :].astype(jnp.float32)
    return total


def fold_spread(value, members, copies, after=()):
    rows, lanes = value.shape[0] // members, value.shape[1]

    def body(*refs):
        total = fold(refs[0], members).astype(jnp.bfloat16)
        for at in range(copies):
            refs[-1][at * rows : (at + 1) * rows, :] = total

    return call(body, half(copies * rows, lanes), [VM] + [HB] * len(after))(value, *after)


def finish_body(factor, spot, mine, other, own, neigh):
    height, lanes = own.shape[0], mine.shape[1]
    for at in range(2):
        rows, columns = slice(at * height, (at + 1) * height), slice(at * lanes, (at + 1) * lanes)
        first = mine[rows, :].astype(jnp.float32) * factor
        second = other[rows, :].astype(jnp.float32) * factor
        own[:, columns] = jnp.where(spot[0] == 0, first, second)
        neigh[:, columns] = jnp.where(spot[0] == 0, second, first)


def output_body(came, held, degree, features, self_weight, neigh_weight, out):
    sums = came[...].astype(jnp.float32) + held[...]
    aggregate = (sums / column(degree, out.shape[1])).astype(jnp.bfloat16)
    out[...] = (
        dot(features[...], self_weight[...], 1, 0) + dot(aggregate, neigh_weight[...], 1, 0)
    ).astype(jnp.bfloat16)


def feature_body(low, high, mid, cotangent, self_weight, out):
    spread = mid[...] + low[...].astype(jnp.float32) + high[...].astype(jnp.float32)
    out[...] = (dot(cotangent[...], self_weight[...], 1, 1) + spread).astype(jnp.bfloat16)


def passed_along(value, steps):
    count = lax.axis_size(ROW)
    leading, last = max(0, -steps), min(count, count - steps)
    return lax.ppermute(value, ROW, [(source, source + steps) for source in range(leading, last)])


def crossed(value, axis, flip):
    return lax.ppermute(value, axis, [(at, at ^ flip) for at in range(lax.axis_size(axis))])


def exchange(value, axes):
    return lax.all_to_all(value, axes, 0, 0, tiled=True)


def local(
    features, self_weight, neigh_weight, tiles, tile_rows, tile_bands, tile_count, degree, cotangent
):
    ncol = lax.axis_size("y")
    near, far = lax.axis_size(NEAR), lax.axis_size("z")
    blk, width = features.shape
    lanes = width // 2
    slots = tiles.shape[2]
    tile_set = tiles[0, 0]
    rows, bands, count = tile_rows[0, 0], tile_bands[0, 0], tile_count[0]
    core, at_col = lax.axis_index("core"), lax.axis_index("y")
    spot = jnp.stack([core, at_col & 1, at_col >> 2, (at_col >> 1) & 1]).astype(jnp.int32)
    degree = degree[None, :]
    factor = 1.0 / math.sqrt(lax.axis_size(ROW) * ncol * blk)

    below, above = passed_along(features, 2), passed_along(features, -2)
    table = jax.ShapeDtypeStruct((slots,), jnp.int32)
    given = [
        pltpu.with_memory_space_constraint(item, pltpu.HBM)
        for item in (degree, cotangent, rows, bands)
    ]
    copies, rows, bands = call(
        share_body,
        [half(ncol * blk, width), table, table],
        [HB] * 4,
        scratch=[
            pltpu.VMEM((1, blk), jnp.int32),
            pltpu.VMEM((blk, width), jnp.bfloat16),
            pltpu.VMEM((blk, width), jnp.bfloat16),
            pltpu.SemaphoreType.DMA((4 + ncol,)),
        ],
        out_specs=[HB, VM, VM],
    )(*given)
    shares = exchange(copies, "y")
    pair = call(pair_body, half(2 * blk, width), [SM] + [VM] * 3)(spot, features, below, above)
    pair = crossed(pair, "core", 1)
    partial, sent, kept = call(
        forward_body,
        [half(ncol * blk, width)] + [half(ncol // 2 * blk, width)] * 2,
        [SM] * 4 + [VM] * 5,
        scratch=[
            pltpu.VMEM((WIDE, blk, width), jnp.bfloat16),
            pltpu.VMEM((ncol + 1, blk, width), jnp.float32),
        ],
        cost=cost(4 * 10**9, tile_set.size * 2 + 21 * features.size * 2),
    )(rows, bands, count, spot, tile_set, below, pair, features, above)

    grads = call(
        grads_body,
        half(4 * width, lanes),
        [VM] * 4,
        cost=cost(2 * (ncol + 1) * blk * width * width, 18 * features.size * 2),
    )(features, cotangent, partial, shares)
    scattered = exchange(grads, NEAR)

    far0, near_landed, own, far1, sent = call(
        backward_body,
        [half(blk, width), half(2 * blk, width), half(blk, width), half(blk, width)]
        + [half(*sent.shape)],
        [SM] * 3 + [VM] * 3 + [HB] * 2,
        out_specs=[VM] * 4 + [HB],
        aliases={7: 4},
        scratch=[pltpu.VMEM((WIDE + 1, blk, width), jnp.float32)],
        cost=cost(5 * 10**9, tile_set.size * 2 + 13 * features.size * 2),
    )(rows, bands, count, tile_set, shares, neigh_weight, grads, sent)
    came = crossed(sent, "y", 1)
    near_landed = crossed(near_landed, "core", 1)
    sent, kept = call(
        halve_body(blk, 2),
        [half(ncol // 4 * blk, width), full(ncol // 4 * blk, width)],
        [SM] + [VM] * 2,
    )(spot, came, kept)
    low, high, mid = call(
        merge_body, [half(blk, width)] * 2 + [full(blk, width)], [SM] + [VM] * 4
    )(spot, near_landed, far0, far1, own)

    joined = fold_spread(scattered, near, far, after=[low])
    joined = exchange(joined, "z")

    came = crossed(sent, "y", 4)
    low, high = passed_along(low, -2), passed_along(high, 2)
    grads = fold_spread(joined, far, near // 2, after=[sent])
    mine = exchange(grads, PLANE)
    other = crossed(mine, "core", 1)

    sent, kept = call(
        halve_body(blk, 3),
        [half(blk, width), full(blk, width)],
        [SM] + [VM] * 2 + [HB],
        cost=cost(2 * 10**9, 0),
    )(spot, came, kept, grads)
    feature_grad = call(feature_body, half(blk, width), [VM] * 5, cost=cost(4 * 10**9, 0))(
        low, high, mid, cotangent, self_weight
    )
    came = crossed(sent, "y", 2)
    output = call(output_body, half(blk, width), [VM] * 6, cost=cost(2 * 10**9, 0))(
        came, kept, degree, features, self_weight, neigh_weight
    )
    self_grad, neigh_grad = call(
        functools.partial(finish_body, factor), [full(width, width)] * 2, [SM] + [VM] * 2
    )(spot, mine, other)
    return (output, feature_grad, self_grad, neigh_grad)


def solution(mesh):
    fine = Mesh(
        np.array(mesh.devices).reshape(mesh.shape["row"] // 8, 4, 2, mesh.shape["col"]),
        ROW + ("y",),
    )
    nodes = ROW + ("y",)
    in_specs = (
        P(nodes, None),
        P(),
        P(),
        P(ROW, "y", None, None, None),
        P(ROW, "y", None),
        P(ROW, "y", None),
        P(ROW, "y"),
        P(nodes),
        P(nodes, None),
    )
    out_specs = (P(nodes, None), P(nodes, None), P(), P())
    return jax.shard_map(local, mesh=fine, in_specs=in_specs, out_specs=out_specs, check_vma=False)
```
